256 devices in a mesh: leaf: 32 (over x, z), row: 4 (over y), col: 2 (over core).
Axes of the slice: x: 4, y: 4, z: 8, core: 2. Of those that a mesh axis runs over, the one named last changes fastest.
Arguments:
- loads: float32 [3, 8192, 2, 256], P(None, ('leaf', 'row', 'col')), may hold values from -6 to 6
- pivot_root: float32 [2, 32, 4, 2, 32, 8192], P(None, None, 'row', 'col', None, 'leaf'), may hold values from -0.046875 to 0.046875
- pivot_mid: float32 [2, 16, 4, 2, 32, 8192], P(None, None, 'row', 'col', None, 'leaf'), may hold values from -0.0625 to 0.0625
- pivot_low: float32 [2, 8, 4, 2, 32, 8192], P(None, None, 'row', 'col', None, 'leaf'), may hold values from -0.09375 to 0.09375
- upper_mid: float32 [2, 16, 4, 2, 32, 8192], P(None, None, 'row', 'col', None, 'leaf'), may hold values from -0.0625 to 0.0625
- upper_low: float32 [2, 8, 4, 2, 32, 8192], P(None, None, 'row', 'col', None, 'leaf'), may hold values from -0.09375 to 0.09375
- lower_mid: float32 [2, 16, 4, 2, 32, 8192], P(None, None, 'row', 'col', None, 'leaf'), may hold values from -0.0625 to 0.0625
- lower_low: float32 [2, 8, 4, 2, 32, 8192], P(None, None, 'row', 'col', None, 'leaf'), may hold values from -0.09375 to 0.09375
- index_maps: int32 [2, 8192], P(None, ('leaf', 'row', 'col')), may hold values from 0 to 8191, as said below
Outputs:
- solution: float32 [3, 8192, 2, 256], P(None, ('leaf', 'row', 'col'))
The draws below stay inside these ranges and needn't reach their ends.
Inputs may be any that keep to these rules, and one draw needn't show every extreme that they name: `index_maps`: row g of a child front lies in block d = g // 32; write d = i * 4 * 2 + c and let G be 32 / 2 for map 0 and 8 for map 1. Its parent row lies in the parent's block (i mod 2G) * 4 * 2 + c or ((i xor G) mod 2G) * 4 * 2 + c, and the parent rows of the rows of one block are distinct.
All inputs are finite; a program needn't handle non-finite values.
Results may differ from the reference program's by a relative error of at most 0.00013.
Values sent between devices are 32-bit elements; how exact they have to be, the bound alone decides.
No kernel may reach another device: no remote copies, remote signals or barrier semaphores. Data moves between devices by JAX's collectives and lax.ppermute only.
A program may use at most 64 MiB of HBM per device.

```python
import jax
import jax.numpy as jnp
from jax import lax

SEP = 8192
LOADS = 256
LEVELS = 3
ROWS = 32
N_LEAF = 32
N_ROW = 4
N_COL = 2


def pick_slots(single, rows):
    first_key, second_key = jax.random.split(single)
    pool = jax.random.permutation(first_key, 2 * rows - 2)[:rows - 2].astype(jnp.int32)
    mapped = jnp.where(pool + 1 < rows - 1, pool + 1, pool + 2)
    fixed = jnp.array([0, rows - 1], dtype=jnp.int32)
    joined = jnp.concatenate([mapped, fixed])
    order = jax.random.permutation(second_key, rows)
    return joined[order].astype(jnp.int32)


def draw_index_maps(key, part):
    cells = N_ROW * N_COL
    blocks = N_LEAF * cells
    rows = SEP // blocks
    block_ids = jnp.arange(blocks, dtype=jnp.int32)
    leaf_ids = block_ids // cells
    cell_ids = block_ids % cells
    results = []
    for which in range(2):
        group = N_LEAF // (2 * (which + 1))
        own_block = leaf_ids % (2 * group) * cells + cell_ids
        other_block = jnp.bitwise_xor(leaf_ids, group) % (2 * group) * cells + cell_ids
        keys = jax.random.split(jax.random.fold_in(key, 17 + which), blocks)
        picks = jax.vmap(lambda single: pick_slots(single, rows))(keys).astype(jnp.int32)
        chosen = jnp.where(picks < rows, own_block[:, None], other_block[:, None])
        results.append((chosen * rows + picks % rows).reshape(SEP))
    return jnp.stack(results).astype(jnp.int32)


def steps_of(own_key, shape, cuts, low, top_value):
    factor_of = 1.0
    for axis_at, blocks in cuts:
        steps = jax.random.uniform(jax.random.fold_in(jax.random.fold_in(own_key, 6), axis_at), (blocks,), jnp.float32, low / len(cuts), top_value / len(cuts))
        factor_of = factor_of * jnp.repeat(jnp.exp(steps), shape[axis_at] // blocks).reshape((-1,) + (1,) * (len(shape) - 1 - axis_at))
    return factor_of


def scatter_about(stream_key, extent, scale, bound, cuts=(), held_as=jnp.bfloat16):
    drawn = jax.random.normal(stream_key, extent, jnp.float32) * scale
    if len(cuts) > 0:
        drawn = steps_of(stream_key, extent, cuts, -0.22, 0.18) * drawn
    return jnp.clip(drawn, min=-bound, max=bound).astype(held_as)


def setup_inputs(seed: int = 0) -> dict:
    splits = jax.random.split(jax.random.key(seed), 10)
    loads = scatter_about(splits[0], (LEVELS, SEP, 2, LOADS), 1.0, 6.0, ((1, 256),), jnp.float32)
    pivot_root = scatter_about(splits[1], (2, N_LEAF, N_ROW, N_COL, ROWS, SEP), (2 * SEP) ** -0.5, 0.046875, ((2, 4), (3, 2), (5, 32)), jnp.float32)
    pivot_mid = scatter_about(splits[2], (2, N_LEAF // 2, N_ROW, N_COL, ROWS, SEP), SEP ** -0.5, 0.0625, ((2, 4), (3, 2), (5, 32)), jnp.float32)
    pivot_low = scatter_about(splits[3], (2, N_LEAF // 4, N_ROW, N_COL, ROWS, SEP), (SEP // 2) ** -0.5, 0.09375, ((2, 4), (3, 2), (5, 32)), jnp.float32)
    upper_mid = scatter_about(splits[4], (2, N_LEAF // 2, N_ROW, N_COL, ROWS, SEP), SEP ** -0.5, 0.0625, ((2, 4), (3, 2), (5, 32)), jnp.float32)
    upper_low = scatter_about(splits[5], (2, N_LEAF // 4, N_ROW, N_COL, ROWS, SEP), (SEP // 2) ** -0.5, 0.09375, ((2, 4), (3, 2), (5, 32)), jnp.float32)
    lower_mid = scatter_about(splits[6], (2, N_LEAF // 2, N_ROW, N_COL, ROWS, SEP), SEP ** -0.5, 0.0625, ((2, 4), (3, 2), (5, 32)), jnp.float32)
    lower_low = scatter_about(splits[7], (2, N_LEAF // 4, N_ROW, N_COL, ROWS, SEP), (SEP // 2) ** -0.5, 0.09375, ((2, 4), (3, 2), (5, 32)), jnp.float32)
    index_maps = draw_index_maps(jax.random.fold_in(splits[9], 71), 0)
    return dict(loads=loads, pivot_root=pivot_root, pivot_mid=pivot_mid, pivot_low=pivot_low, upper_mid=upper_mid, upper_low=upper_low, lower_mid=lower_mid, lower_low=lower_low, index_maps=index_maps)


def conj_apply(matrix, vector):
    contract = (((0,), (0,)), ((), ()))

    def product(left, right):
        return lax.dot_general(left, right, contract, precision=lax.Precision.HIGHEST, preferred_element_type=jnp.float32)

    real_part = product(matrix[0], vector[:, 0, :]) + product(matrix[1], vector[:, 1, :])
    imag_part = product(matrix[0], vector[:, 1, :]) - product(matrix[1], vector[:, 0, :])
    return jnp.stack([real_part, imag_part], axis=1)


def level_apply(matrix, vector, level):
    width = SEP // (2 ** level)
    count = 2 ** level
    blocks = matrix.reshape(2, width, count, width)
    pieces = [conj_apply(blocks[:, :, front, :], vector[front * width:(front + 1) * width]) for front in range(count)]
    return jnp.concatenate(pieces, axis=0)


def reference(loads, pivot_root, pivot_mid, pivot_low, upper_mid, upper_low, lower_mid, lower_low, index_maps):
    positions = jnp.arange(SEP, dtype=jnp.int32)
    width_mid = SEP // 2
    width_low = SEP // 4
    target_mid = index_maps[0].astype(jnp.int32)
    target_low = ((positions // width_low) // 2) * width_mid + index_maps[1].astype(jnp.int32)
    inner_low = level_apply(pivot_low, loads[2], 2)
    update_low = level_apply(upper_low, inner_low, 2)
    right_mid = loads[1] - jnp.zeros_like(loads[1]).at[target_low].add(update_low)
    inner_mid = level_apply(pivot_mid, right_mid, 1)
    update_mid = level_apply(upper_mid, inner_mid, 1)
    right_root = loads[0] - jnp.zeros_like(loads[0]).at[target_mid].add(update_mid)
    inner_root = level_apply(pivot_root, right_root, 0)
    final_mid = inner_mid - level_apply(lower_mid, inner_root[target_mid], 1)
    final_low = inner_low - level_apply(lower_low, final_mid[target_low], 2)
    return jnp.stack([inner_root, final_mid, final_low])
```

```python
import jax
import jax.numpy as jnp
from jax import lax
from jax.sharding import PartitionSpec as P

NEAR = 8


def product(left, right):
    contract = (((0,), (0,)), ((), ()))
    return lax.dot_general(
        left,
        right,
        contract,
        precision=lax.Precision.HIGH,
        preferred_element_type=jnp.float32,
    )


def swapped(shard, bit):
    return lax.ppermute(shard, "leaf", [(i, i ^ 1 << bit) for i in range(lax.axis_size("leaf"))])


def shifted(shard, far):
    count = lax.axis_size("leaf")
    return lax.ppermute(shard, "leaf", [(i, (i - far * NEAR) % count) for i in range(count)])


def near_gather(block):
    count = lax.axis_size("leaf")
    groups = [list(range(start, start + NEAR)) for start in range(0, count, NEAR)]
    spread = jnp.broadcast_to(block[None], (NEAR,) + block.shape)
    gathered = lax.all_to_all(spread, "leaf", 0, 0, axis_index_groups=groups)
    return gathered.reshape(NEAR * block.shape[0], block.shape[1])


def conj_apply(matrix, vector):
    half = vector.shape[1] // 2
    turned = jnp.concatenate([vector[:, half:], -vector[:, :half]], axis=1)
    return product(matrix.reshape(-1, matrix.shape[-1]), jnp.concatenate([vector, turned], axis=0))


def cell_scatter(partial):
    row, col = lax.axis_index("row"), lax.axis_index("col")
    rows = lax.axis_size("row")
    parts = partial.reshape(rows, 2, -1, partial.shape[-1])
    theirs = lax.dynamic_index_in_dim(parts, 1 - col, 1, keepdims=False)
    mine = lax.dynamic_index_in_dim(parts, col, 1, keepdims=False)
    summed = mine + lax.ppermute(theirs, "col", [(0, 1), (1, 0)])
    total = lax.dynamic_index_in_dim(summed, row, 0, keepdims=False)
    for step in (2, 1, 3):
        piece = lax.dynamic_index_in_dim(summed, (row + step) % rows, 0, keepdims=False)
        total = total + lax.ppermute(piece, "row", [(i, (i + step) % rows) for i in range(rows)])
    return total


def front_apply(matrix, block, wide):
    local = matrix.reshape(2, wide, -1, matrix.shape[-1])
    gathered = near_gather(block)
    far = lax.axis_index("leaf") // NEAR
    pieces = [(far % wide, gathered)]
    if wide == 2:
        pieces.append(((far + 1) % 2, swapped(gathered, 3)))
    elif wide == 4:
        pieces += [((far + step) % 4, shifted(gathered, step)) for step in (2, 1, 3)]
    partial = None
    for at, vector in pieces:
        term = conj_apply(lax.dynamic_index_in_dim(local, at, 1, keepdims=False), vector)
        partial = term if partial is None else partial + term
    return cell_scatter(partial)


def route_masks(index_block, group, rows):
    leaf_index = lax.axis_index("leaf")
    cell_index = lax.axis_index(("row", "col"))
    cells = lax.axis_size("row") * lax.axis_size("col")
    own_block = leaf_index % (2 * group) * cells + cell_index
    target = index_block // rows
    slot = index_block % rows
    picked = (slot[:, None] == jnp.arange(rows, dtype=jnp.int32)[None, :]).astype(jnp.float32)
    mine = picked * (target == own_block).astype(jnp.float32)[:, None]
    return (mine, picked - mine)


def send_upward(update, masks, group):
    mine, theirs = masks
    to_other = product(theirs, update)
    received = swapped(to_other, group.bit_length() - 1)
    return product(mine, update) + received


def pull_down(parent, masks, group):
    mine, theirs = masks
    other = swapped(parent, group.bit_length() - 1)
    return product(mine.T, parent) + product(theirs.T, other)


def on_device(
    loads, pivot_root, pivot_mid, pivot_low, upper_mid, upper_low, lower_mid, lower_low, index_maps
):
    group_mid = lax.axis_size("leaf") // 2
    group_low = lax.axis_size("leaf") // 4
    levels, rows = loads.shape[:2]
    flat = loads.reshape(levels, rows, -1)
    up_mid = route_masks(index_maps[0], group_mid, rows)
    up_low = route_masks(index_maps[1], group_low, rows)
    inner_low = front_apply(pivot_low, flat[2], 1)
    update_low = front_apply(upper_low, inner_low, 1)
    right_mid = flat[1] - send_upward(update_low, up_low, group_low)
    inner_mid = front_apply(pivot_mid, right_mid, 2)
    update_mid = front_apply(upper_mid, inner_mid, 2)
    right_root = flat[0] - send_upward(update_mid, up_mid, group_mid)
    inner_root = front_apply(pivot_root, right_root, 4)
    final_mid = inner_mid - front_apply(lower_mid, pull_down(inner_root, up_mid, group_mid), 2)
    final_low = inner_low - front_apply(lower_low, pull_down(final_mid, up_low, group_low), 1)
    return jnp.stack([inner_root, final_mid, final_low]).reshape(loads.shape)


def solution(mesh):
    matrix = P(None, None, "row", "col", None, "leaf")
    vectors = P(None, ("leaf", "row", "col"), None, None)
    in_specs = (vectors,) + (matrix,) * 7 + (P(None, ("leaf", "row", "col")),)
    return jax.shard_map(
        on_device, mesh=mesh, in_specs=in_specs, out_specs=vectors, check_vma=False
    )
```

```python
import jax
import jax.numpy as jnp
from jax import lax
from jax.sharding import PartitionSpec as P

NEAR = 8


def product(left, right):
    contract = (((0,), (0,)), ((), ()))
    return lax.dot_general(
        left,
        right,
        contract,
        precision=lax.Precision.HIGH,
        preferred_element_type=jnp.float32,
    )


def swapped(shard, bit):
    return lax.ppermute(shard, "leaf", [(i, i ^ 1 << bit) for i in range(lax.axis_size("leaf"))])


def shifted(shard, far):
    count = lax.axis_size("leaf")
    return lax.ppermute(shard, "leaf", [(i, (i - far * NEAR) % count) for i in range(count)])


def near_block(block, step):
    count = lax.axis_size("leaf")
    pairs = [(i // NEAR * NEAR + (i + step) % NEAR, i) for i in range(count)]
    return lax.ppermute(block, "leaf", pairs)


def near_gather(block):
    above, below = near_block(block, 2), near_block(block, -2)
    across = near_block(above, 2)
    rows = block.shape[0]
    up = near_block(jnp.concatenate([block, above]), 1)
    down = near_block(jnp.concatenate([block, below]), -1)
    ring = [block, up[:rows], above, up[rows:], across, down[rows:], below, down[:rows]]
    twice = jnp.concatenate(ring + ring)
    start = (NEAR - lax.axis_index("leaf") % NEAR) % NEAR * rows
    return lax.dynamic_slice_in_dim(twice, start, NEAR * rows)


def conj_apply(matrix, vector):
    half = vector.shape[1] // 2
    turned = jnp.concatenate([vector[:, half:], -vector[:, :half]], axis=1)
    return product(matrix.reshape(-1, matrix.shape[-1]), jnp.concatenate([vector, turned], axis=0))


def cell_scatter(partial):
    row, col = lax.axis_index("row"), lax.axis_index("col")
    rows = lax.axis_size("row")
    parts = partial.reshape(rows, 2, -1, partial.shape[-1])
    theirs = lax.dynamic_index_in_dim(parts, 1 - col, 1, keepdims=False)
    mine = lax.dynamic_index_in_dim(parts, col, 1, keepdims=False)
    summed = mine + lax.ppermute(theirs, "col", [(0, 1), (1, 0)])
    total = lax.dynamic_index_in_dim(summed, row, 0, keepdims=False)
    for step in (2, 1, 3):
        piece = lax.dynamic_index_in_dim(summed, (row + step) % rows, 0, keepdims=False)
        total = total + lax.ppermute(piece, "row", [(i, (i + step) % rows) for i in range(rows)])
    return total


def front_apply(matrix, block, wide):
    local = matrix.reshape(2, wide, -1, matrix.shape[-1])
    gathered = near_gather(block)
    far = lax.axis_index("leaf") // NEAR
    pieces = [(far % wide, gathered)]
    if wide == 2:
        pieces.append(((far + 1) % 2, swapped(gathered, 3)))
    elif wide == 4:
        pieces += [((far + step) % 4, shifted(gathered, step)) for step in (2, 1, 3)]
    partial = None
    for at, vector in pieces:
        term = conj_apply(lax.dynamic_index_in_dim(local, at, 1, keepdims=False), vector)
        partial = term if partial is None else partial + term
    return cell_scatter(partial)


def route_masks(index_block, group, rows):
    leaf_index = lax.axis_index("leaf")
    cell_index = lax.axis_index(("row", "col"))
    cells = lax.axis_size("row") * lax.axis_size("col")
    own_block = leaf_index % (2 * group) * cells + cell_index
    target = index_block // rows
    slot = index_block % rows
    picked = (slot[:, None] == jnp.arange(rows, dtype=jnp.int32)[None, :]).astype(jnp.float32)
    mine = picked * (target == own_block).astype(jnp.float32)[:, None]
    return (mine, picked - mine)


def send_upward(update, masks, group):
    mine, theirs = masks
    to_other = product(theirs, update)
    received = swapped(to_other, group.bit_length() - 1)
    return product(mine, update) + received


def pull_down(parent, masks, group):
    mine, theirs = masks
    other = swapped(parent, group.bit_length() - 1)
    return product(mine.T, parent) + product(theirs.T, other)


def on_device(
    loads, pivot_root, pivot_mid, pivot_low, upper_mid, upper_low, lower_mid, lower_low, index_maps
):
    group_mid = lax.axis_size("leaf") // 2
    group_low = lax.axis_size("leaf") // 4
    levels, rows = loads.shape[:2]
    flat = loads.reshape(levels, rows, -1)
    up_mid = route_masks(index_maps[0], group_mid, rows)
    up_low = route_masks(index_maps[1], group_low, rows)
    inner_low = front_apply(pivot_low, flat[2], 1)
    update_low = front_apply(upper_low, inner_low, 1)
    right_mid = flat[1] - send_upward(update_low, up_low, group_low)
    inner_mid = front_apply(pivot_mid, right_mid, 2)
    update_mid = front_apply(upper_mid, inner_mid, 2)
    right_root = flat[0] - send_upward(update_mid, up_mid, group_mid)
    inner_root = front_apply(pivot_root, right_root, 4)
    final_mid = inner_mid - front_apply(lower_mid, pull_down(inner_root, up_mid, group_mid), 2)
    final_low = inner_low - front_apply(lower_low, pull_down(final_mid, up_low, group_low), 1)
    return jnp.stack([inner_root, final_mid, final_low]).reshape(loads.shape)


def solution(mesh):
    matrix = P(None, None, "row", "col", None, "leaf")
    vectors = P(None, ("leaf", "row", "col"), None, None)
    in_specs = (vectors,) + (matrix,) * 7 + (P(None, ("leaf", "row", "col")),)
    return jax.shard_map(
        on_device, mesh=mesh, in_specs=in_specs, out_specs=vectors, check_vma=False
    )
```

```python
import functools

import jax
import jax.numpy as jnp
from jax import lax
from jax.experimental import pallas as pl
from jax.experimental.pallas import tpu as pltpu
from jax.sharding import PartitionSpec as P

NEAR = 8
UNIT = 64
GROUP = 2 * UNIT


def core_swapped(shard):
    return lax.ppermute(shard, "col", [(0, 1), (1, 0)])


def far_swapped(shard, flip):
    return lax.ppermute(shard, "leaf", [(i, i ^ flip * NEAR) for i in range(lax.axis_size("leaf"))])


def near_block(block, step):
    count = lax.axis_size("leaf")
    pairs = [(i // NEAR * NEAR + (i + step) % NEAR, i) for i in range(count)]
    return lax.ppermute(block, "leaf", pairs)


def beside(own, other, upper):
    return jnp.where(
        upper,
        jnp.concatenate([other, own], axis=-1),
        jnp.concatenate([own, other], axis=-1),
    )


def lane_halves(block, upper):
    half = block.shape[-1] // 2
    lower, higher = block[..., :half], block[..., half:]
    return jnp.where(upper, higher, lower), jnp.where(upper, lower, higher)


def split(value):
    high = value.astype(jnp.bfloat16)
    return high, (value - high.astype(jnp.float32)).astype(jnp.bfloat16)


def dot(left, right):
    return lax.dot_general(
        left, right, (((0,), (0,)), ((), ())), preferred_element_type=jnp.float32
    )


def turned(value):
    parts = []
    for at in range(0, value.shape[1], GROUP):
        parts += [value[:, at + UNIT : at + GROUP], -value[:, at : at + UNIT]]
    return jnp.concatenate(parts, axis=1)


def apply_kernel(counts, place_ref, *refs):
    wide, pieces = len(counts), refs[:6]
    mine_ref, theirs_ref, vector, result = refs[-4:]
    starts = [6 + sum(counts[:flip]) for flip in range(wide)]
    near, far, row, core = (place_ref[i] for i in range(4))
    rows = vector.shape[0] // (wide * NEAR)
    steps = [(0, 0, 0), (1, 1, 0), (1, 3, 1), (2, 2, 0), (3, 4, 0), (4, 7, 0), (4, 5, 1), (5, 6, 0)]
    for piece, step, part in steps:
        block = (near + step) % NEAR
        for flip in range(wide):
            at = ((far ^ flip) % wide * NEAR + block) * rows
            base = (part * wide + flip) * rows
            vector[pl.ds(pl.multiple_of(at, rows), rows), :] = pieces[piece][base : base + rows, :]
    sums = [None] * wide
    straight = vector[...]
    for part, value in ((0, straight), (1, turned(straight))):
        high, low = split(value)
        for flip in range(wide):
            at = starts[flip]
            factor = refs[at][part] if counts[flip] == 1 else refs[at + part][0]
            top, rest = split(factor)
            term = dot(top, high) + dot(top, low) + dot(rest, high)
            sums[flip] = term if sums[flip] is None else sums[flip] + term
    for flip in range(wide):
        for at in range(8):
            result[at // 2, at % 2, flip * rows : (flip + 1) * rows, :] = sums[flip][
                at * rows : (at + 1) * rows
            ]
    for step in range(4):
        mine_ref[step] = result[(row + step) % 4, core]
        theirs_ref[step] = result[(row + step) % 4, 1 - core]


def local_apply(factors, pieces, place, wide):
    rows, lanes = pieces[0].shape
    whole = pl.BlockSpec(memory_space=pltpu.VMEM)
    counts = [len(factor) for factor in factors]
    arrays = [array for factor in factors for array in factor]
    return pl.pallas_call(
        functools.partial(apply_kernel, counts),
        out_shape=[jax.ShapeDtypeStruct((4, rows, lanes), jnp.float32)] * 2,
        in_specs=[pl.BlockSpec(memory_space=pltpu.SMEM)] + [whole] * (6 + len(arrays)),
        out_specs=[whole] * 2,
        scratch_shapes=[
            pltpu.VMEM((arrays[0].shape[1], lanes), jnp.float32),
            pltpu.VMEM((4, 2, rows, lanes), jnp.float32),
        ],
        compiler_params=pltpu.CompilerParams(vmem_limit_bytes=32 * 2**20),
    )(place, *pieces, *arrays)


def front_apply(factors, block, place, wide):
    above, below = near_block(block, 2), near_block(block, -2)
    up = near_block(jnp.concatenate([block, above]), 1)
    down = near_block(jnp.concatenate([block, below]), -1)
    across = near_block(above, 2)
    mine, theirs = local_apply(factors, [block, up, above, across, down, below], place, wide)
    summed = mine + core_swapped(theirs)
    rows = lax.axis_size("row")
    total = summed[0]
    for step in (1, 3, 2):
        total = total + lax.ppermute(
            summed[step], "row", [(i, (i + step) % rows) for i in range(rows)]
        )
    return total


def routed(mask, value, axis):
    return lax.dot_general(
        mask,
        value,
        (((axis,), (0,)), ((), ())),
        precision=lax.Precision.HIGH,
        preferred_element_type=jnp.float32,
    )


def chosen(upper, first, second):
    return jnp.where(jnp.full(first.shape, upper, jnp.int32) == 1, first, second)


def mask_into(mask_ref, entries, place_ref, group, flip):
    leaf, cell = place_ref[4], place_ref[5]
    size, rows = mask_ref.shape[0], entries[0].shape[1]
    every = lax.broadcasted_iota(jnp.int32, (size, rows), 0)
    for side, entry in enumerate(entries):
        own_block = lax.rem(leaf ^ side * NEAR, 2 * group) * 8 + cell
        target, slot = lax.div(entry, rows), lax.rem(entry, rows)
        at = jnp.where(target == own_block, side * rows, (side ^ flip) * rows) + slot
        hit = jnp.broadcast_to(at, (size, rows)) == every
        mask_ref[:, side * rows : (side + 1) * rows] = jnp.where(hit, 1.0, 0.0).astype(jnp.float32)


def first_kernel(place_ref, loads_ref, maps_ref, low_ref, kept_ref, gone_ref):
    rows, columns = loads_ref.shape[1], loads_ref.shape[3]
    odd = place_ref[1] & 1
    for level in range(3):
        real, imag = loads_ref[level, :, 0, :], loads_ref[level, :, 1, :]
        parts = []
        for at in range(0, columns, UNIT):
            parts += [real[:, at : at + UNIT], imag[:, at : at + UNIT]]
        whole = jnp.concatenate(parts, axis=1)
        if level == 2:
            low_ref[...] = whole
        else:
            lower, upper = whole[:, :columns], whole[:, columns:]
            kept_ref[level * rows : (level + 1) * rows, :] = chosen(odd, upper, lower)
            gone_ref[level * rows : (level + 1) * rows, :] = chosen(odd, lower, upper)
    gone_ref[2 * rows :, :] = jnp.zeros((8, columns), jnp.float32)
    gone_ref[2 * rows : 2 * rows + 2, :rows] = maps_ref[...].astype(jnp.float32)


def second_kernel(place_ref, maps_ref, kept_ref, got_ref, mid_ref, mask_ref, kept2_ref, gone_ref):
    rows, lanes = maps_ref.shape[1], kept_ref.shape[1] // 2
    high = place_ref[1] >> 1
    mid_ref[:rows, :] = kept_ref[rows:, :]
    mid_ref[rows:, :] = got_ref[rows : 2 * rows, :]
    other = got_ref[2 * rows : 2 * rows + 2, :rows].astype(jnp.int32)
    mask_into(mask_ref, [maps_ref[1:2, :], other[1:2]], place_ref, NEAR, 1)
    for half, source in enumerate((kept_ref, got_ref)):
        lower, upper = source[:rows, :lanes], source[:rows, lanes:]
        kept2_ref[half * rows : (half + 1) * rows, :] = chosen(high, upper, lower)
        gone_ref[half * rows : (half + 1) * rows, :] = chosen(high, lower, upper)
    gone_ref[2 * rows :, :] = jnp.zeros((8, lanes), jnp.float32)
    gone_ref[2 * rows : 2 * rows + 1, :rows] = maps_ref[0:1, :].astype(jnp.float32)
    gone_ref[2 * rows + 1 : 2 * rows + 2, :rows] = other[0:1].astype(jnp.float32)


def third_kernel(place_ref, maps_ref, kept_ref, got1_ref, got2_ref, root_ref, mask_ref):
    rows = maps_ref.shape[1]
    root_ref[: 2 * rows, :] = kept_ref[...]
    root_ref[2 * rows :, :] = got2_ref[: 2 * rows, :]
    one = got1_ref[2 * rows : 2 * rows + 1, :rows].astype(jnp.int32)
    rest = got2_ref[2 * rows : 2 * rows + 2, :rows].astype(jnp.int32)
    entries = [maps_ref[0:1, :], one, rest[0:1], rest[1:2]]
    mask_into(mask_ref, entries, place_ref, 2 * NEAR, 2)


def last_kernel(root_ref, mid_ref, low_ref, out_ref):
    for level, source in enumerate((root_ref, mid_ref, low_ref)):
        for at in range(0, source.shape[1], GROUP):
            column = at // 2
            out_ref[level, :, 0, column : column + UNIT] = source[:, at : at + UNIT]
            out_ref[level, :, 1, column : column + UNIT] = source[:, at + UNIT : at + GROUP]


def small(kernel, shapes, place, *arrays):
    whole = pl.BlockSpec(memory_space=pltpu.VMEM)
    scalars = [] if place is None else [pl.BlockSpec(memory_space=pltpu.SMEM)]
    operands = arrays if place is None else (place, *arrays)
    return pl.pallas_call(
        kernel,
        out_shape=[jax.ShapeDtypeStruct(shape, jnp.float32) for shape in shapes],
        in_specs=scalars + [whole] * len(arrays),
        out_specs=[whole] * len(shapes),
        compiler_params=pltpu.CompilerParams(vmem_limit_bytes=16 * 2**20),
    )(*operands)


def on_device(
    loads, pivot_root, pivot_mid, pivot_low, upper_mid, upper_low, lower_mid, lower_low, index_maps
):
    levels, rows, _, columns = loads.shape
    leaf, core, row = lax.axis_index("leaf"), lax.axis_index("col"), lax.axis_index("row")
    cell = lax.axis_index(("row", "col"))
    far = leaf >> 3
    odd, high = far & 1 == 1, far & 2 == 2
    place = jnp.stack([leaf & NEAR - 1, far, row, core, leaf, cell]).astype(jnp.int32)
    barrier = lax.optimization_barrier

    def local(matrix):
        return matrix.reshape(2, -1, matrix.shape[-1])

    shapes = [(rows, 2 * columns), (2 * rows, columns), (2 * rows + 8, columns)]
    load_low, kept, gone = small(first_kernel, shapes, place, loads, index_maps)
    load_low, odd, high = barrier((load_low, odd, high))
    got = far_swapped(gone, 1)
    half = columns // 2
    shapes = [(2 * rows, columns), (2 * rows, 2 * rows), (2 * rows, half), (2 * rows + 8, half)]
    load_mid, low_mask, kept, gone = small(second_kernel, shapes, place, index_maps, kept, got)

    own_pivot, own_upper, own_lower = local(pivot_mid), local(upper_mid), local(lower_mid)
    root = local(pivot_root)
    got, own_pivot, root = barrier((got, own_pivot, root))
    far_pivot = far_swapped(own_pivot, 1)
    three_real, one_real = far_swapped(root[:1], 3), far_swapped(root[:1], 1)
    three_imag = far_swapped(root[1:], 3)

    inner_low = front_apply([[local(pivot_low)]], load_low, place, 1)
    ready = (inner_low, load_mid, far_pivot, three_real)
    inner_low, load_mid, far_pivot, three_real = barrier(ready)
    update_low = front_apply([[local(upper_low)]], inner_low, place, 1)
    update_low, one_real, three_imag = barrier((update_low, one_real, three_imag))
    stays, goes = lane_halves(update_low, odd)
    update = jnp.concatenate([stays, far_swapped(goes, 1)])
    right_mid = load_mid - routed(low_mask, update, 1)
    right_mid, gone = barrier((right_mid, gone))
    got_root = far_swapped(gone, 2)
    got_root, late_root, one_real = barrier((got_root, root[1:], one_real))
    one_imag, two_real = far_swapped(late_root, 1), far_swapped(one_real, 3)
    one_imag, own_upper = barrier((one_imag, own_upper))
    far_upper, two_imag = far_swapped(own_upper, 1), far_swapped(one_imag, 3)
    shapes = [(4 * rows, half), (4 * rows, 4 * rows)]
    load_root, root_mask = small(third_kernel, shapes, place, index_maps, kept, got, got_root)
    inner_mid = front_apply([[own_pivot], [far_pivot]], right_mid, place, 2)
    inner_mid, one_imag, two_real = barrier((inner_mid, one_imag, two_real))
    update_mid = front_apply([[own_upper], [far_upper]], inner_mid, place, 2)
    update_mid, two_imag, load_root = barrier((update_mid, two_imag, load_root))
    stays, goes = lane_halves(update_mid, high)
    update = jnp.concatenate([stays, far_swapped(goes, 2)])
    right_root = load_root - routed(root_mask, update, 1)
    right_root, own_lower = barrier((right_root, own_lower))
    far_lower = far_swapped(own_lower, 1)
    inner_root = front_apply(
        [[root], [one_real, one_imag], [two_real, two_imag], [three_real, three_imag]], right_root, place, 4
    )
    inner_root, far_lower = barrier((inner_root, far_lower))

    z_root = routed(root_mask, inner_root, 0)
    own = jnp.concatenate([z_root[: 2 * rows], inner_root[: 2 * rows]])
    other = jnp.concatenate([z_root[2 * rows :], inner_root[2 * rows :]])
    halves = beside(own, far_swapped(other, 2), high)
    z_mid, root_half = halves[: 2 * rows], halves[2 * rows :]
    final_mid = inner_mid - front_apply([[own_lower], [far_lower]], z_mid, place, 2)

    z_half = routed(low_mask, final_mid, 0)
    own = jnp.concatenate([z_half[:rows], final_mid[:rows], root_half[:rows]])
    other = jnp.concatenate([z_half[rows:], final_mid[rows:], root_half[rows:]])
    wholes = beside(own, far_swapped(other, 1), odd)
    final_low = inner_low - front_apply([[local(lower_low)]], wholes[:rows], place, 1)
    finals = (wholes[2 * rows :], wholes[rows : 2 * rows], final_low)
    return small(last_kernel, [loads.shape], None, *finals)[0]


def solution(mesh):
    matrix = P(None, None, "row", "col", None, "leaf")
    vectors = P(None, ("leaf", "row", "col"), None, None)
    in_specs = (vectors,) + (matrix,) * 7 + (P(None, ("leaf", "row", "col")),)
    return jax.shard_map(
        on_device, mesh=mesh, in_specs=in_specs, out_specs=vectors, check_vma=False
    )
```

```python
import functools

import jax
import jax.numpy as jnp
from jax import lax
from jax.experimental import pallas as pl
from jax.experimental.pallas import tpu as pltpu
from jax.sharding import PartitionSpec as P

NEAR = 8
UNIT = 64
GROUP = 2 * UNIT


def core_swapped(shard):
    return lax.ppermute(shard, "col", [(0, 1), (1, 0)])


def far_swapped(shard, flip):
    return lax.ppermute(shard, "leaf", [(i, i ^ flip * NEAR) for i in range(lax.axis_size("leaf"))])


def near_block(block, step):
    count = lax.axis_size("leaf")
    pairs = [(i // NEAR * NEAR + (i + step) % NEAR, i) for i in range(count)]
    return lax.ppermute(block, "leaf", pairs)


def beside(own, other, upper):
    return jnp.where(
        upper,
        jnp.concatenate([other, own], axis=-1),
        jnp.concatenate([own, other], axis=-1),
    )


def lane_halves(block, upper):
    half = block.shape[-1] // 2
    lower, higher = block[..., :half], block[..., half:]
    return jnp.where(upper, higher, lower), jnp.where(upper, lower, higher)


def split(value):
    high = value.astype(jnp.bfloat16)
    return high, (value - high.astype(jnp.float32)).astype(jnp.bfloat16)


def dot(left, right):
    return lax.dot_general(
        left, right, (((0,), (0,)), ((), ())), preferred_element_type=jnp.float32
    )


def turned(value):
    parts = []
    for at in range(0, value.shape[1], GROUP):
        parts += [value[:, at + UNIT : at + GROUP], -value[:, at : at + UNIT]]
    return jnp.concatenate(parts, axis=1)


def apply_kernel(counts, place_ref, *refs):
    wide, pieces = len(counts), refs[:6]
    mine_ref, theirs_ref, vector, result = refs[-4:]
    starts = [6 + sum(counts[:flip]) for flip in range(wide)]
    near, far, row, core = (place_ref[i] for i in range(4))
    rows = vector.shape[0] // (wide * NEAR)
    steps = [(0, 0, 0), (1, 1, 0), (1, 3, 1), (2, 2, 0), (3, 4, 0), (4, 7, 0), (4, 5, 1), (5, 6, 0)]
    for piece, step, part in steps:
        block = (near + step) % NEAR
        for flip in range(wide):
            at = ((far ^ flip) % wide * NEAR + block) * rows
            base = (part * wide + flip) * rows
            vector[pl.ds(pl.multiple_of(at, rows), rows), :] = pieces[piece][base : base + rows, :]
    sums = [None] * wide
    straight = vector[...]
    for part, value in ((0, straight), (1, turned(straight))):
        high, low = split(value)
        for flip in range(wide):
            at = starts[flip]
            factor = refs[at][part] if counts[flip] == 1 else refs[at + part][0]
            top, rest = split(factor)
            lanes = high.shape[1]
            if lanes <= 128:
                both = dot(top, jnp.concatenate([high, low], axis=1))
                term = both[:, :lanes] + both[:, lanes:] + dot(rest, high)
            else:
                term = dot(top, high) + dot(top, low) + dot(rest, high)
            sums[flip] = term if sums[flip] is None else sums[flip] + term
    for flip in range(wide):
        for at in range(8):
            result[at // 2, at % 2, flip * rows : (flip + 1) * rows, :] = sums[flip][
                at * rows : (at + 1) * rows
            ]
    for step in range(4):
        mine_ref[step] = result[(row + step) % 4, core]
        theirs_ref[step] = result[(row + step) % 4, 1 - core]


def local_apply(factors, pieces, place, wide):
    rows, lanes = pieces[0].shape
    whole = pl.BlockSpec(memory_space=pltpu.VMEM)
    counts = [len(factor) for factor in factors]
    arrays = [array for factor in factors for array in factor]
    return pl.pallas_call(
        functools.partial(apply_kernel, counts),
        out_shape=[jax.ShapeDtypeStruct((4, rows, lanes), jnp.float32)] * 2,
        in_specs=[pl.BlockSpec(memory_space=pltpu.SMEM)] + [whole] * (6 + len(arrays)),
        out_specs=[whole] * 2,
        scratch_shapes=[
            pltpu.VMEM((arrays[0].shape[1], lanes), jnp.float32),
            pltpu.VMEM((4, 2, rows, lanes), jnp.float32),
        ],
        compiler_params=pltpu.CompilerParams(vmem_limit_bytes=32 * 2**20),
    )(place, *pieces, *arrays)


def front_apply(factors, block, place, wide):
    above, below = near_block(block, 2), near_block(block, -2)
    up = near_block(jnp.concatenate([block, above]), 1)
    down = near_block(jnp.concatenate([block, below]), -1)
    across = near_block(above, 2)
    mine, theirs = local_apply(factors, [block, up, above, across, down, below], place, wide)
    summed = mine + core_swapped(theirs)
    rows = lax.axis_size("row")
    total = summed[0]
    for step in (1, 3, 2):
        total = total + lax.ppermute(
            summed[step], "row", [(i, (i + step) % rows) for i in range(rows)]
        )
    return total


def routed(mask, value, axis):
    return lax.dot_general(
        mask,
        value,
        (((axis,), (0,)), ((), ())),
        precision=lax.Precision.HIGH,
        preferred_element_type=jnp.float32,
    )


def chosen(upper, first, second):
    return jnp.where(jnp.full(first.shape, upper, jnp.int32) == 1, first, second)


def mask_into(mask_ref, entries, place_ref, group, flip):
    leaf, cell = place_ref[4], place_ref[5]
    size, rows = mask_ref.shape[0], entries[0].shape[1]
    every = lax.broadcasted_iota(jnp.int32, (size, rows), 0)
    for side, entry in enumerate(entries):
        own_block = lax.rem(leaf ^ side * NEAR, 2 * group) * 8 + cell
        target, slot = lax.div(entry, rows), lax.rem(entry, rows)
        at = jnp.where(target == own_block, side * rows, (side ^ flip) * rows) + slot
        hit = jnp.broadcast_to(at, (size, rows)) == every
        mask_ref[:, side * rows : (side + 1) * rows] = jnp.where(hit, 1.0, 0.0).astype(jnp.float32)


def first_kernel(place_ref, loads_ref, maps_ref, low_ref, kept_ref, gone_ref):
    rows, columns = loads_ref.shape[1], loads_ref.shape[3]
    odd = place_ref[1] & 1
    for level in range(3):
        real, imag = loads_ref[level, :, 0, :], loads_ref[level, :, 1, :]
        parts = []
        for at in range(0, columns, UNIT):
            parts += [real[:, at : at + UNIT], imag[:, at : at + UNIT]]
        whole = jnp.concatenate(parts, axis=1)
        if level == 2:
            low_ref[...] = whole
        else:
            lower, upper = whole[:, :columns], whole[:, columns:]
            kept_ref[level * rows : (level + 1) * rows, :] = chosen(odd, upper, lower)
            gone_ref[level * rows : (level + 1) * rows, :] = chosen(odd, lower, upper)
    gone_ref[2 * rows :, :] = jnp.zeros((8, columns), jnp.float32)
    gone_ref[2 * rows : 2 * rows + 2, :rows] = maps_ref[...].astype(jnp.float32)


def second_kernel(place_ref, maps_ref, kept_ref, got_ref, mid_ref, mask_ref, kept2_ref, gone_ref):
    rows, lanes = maps_ref.shape[1], kept_ref.shape[1] // 2
    high = place_ref[1] >> 1
    mid_ref[:rows, :] = kept_ref[rows:, :]
    mid_ref[rows:, :] = got_ref[rows : 2 * rows, :]
    other = got_ref[2 * rows : 2 * rows + 2, :rows].astype(jnp.int32)
    mask_into(mask_ref, [maps_ref[1:2, :], other[1:2]], place_ref, NEAR, 1)
    for half, source in enumerate((kept_ref, got_ref)):
        lower, upper = source[:rows, :lanes], source[:rows, lanes:]
        kept2_ref[half * rows : (half + 1) * rows, :] = chosen(high, upper, lower)
        gone_ref[half * rows : (half + 1) * rows, :] = chosen(high, lower, upper)
    gone_ref[2 * rows :, :] = jnp.zeros((8, lanes), jnp.float32)
    gone_ref[2 * rows : 2 * rows + 1, :rows] = maps_ref[0:1, :].astype(jnp.float32)
    gone_ref[2 * rows + 1 : 2 * rows + 2, :rows] = other[0:1].astype(jnp.float32)


def third_kernel(place_ref, maps_ref, kept_ref, got1_ref, got2_ref, root_ref, mask_ref):
    rows = maps_ref.shape[1]
    root_ref[: 2 * rows, :] = kept_ref[...]
    root_ref[2 * rows :, :] = got2_ref[2 * rows : 4 * rows, :]
    one = got1_ref[2 * rows : 2 * rows + 1, :rows].astype(jnp.int32)
    rest = got2_ref[4 * rows : 4 * rows + 2, :rows].astype(jnp.int32)
    entries = [maps_ref[0:1, :], one, rest[0:1], rest[1:2]]
    mask_into(mask_ref, entries, place_ref, 2 * NEAR, 2)


def last_kernel(root_ref, mid_ref, low_ref, out_ref):
    for level, source in enumerate((root_ref, mid_ref, low_ref)):
        for at in range(0, source.shape[1], GROUP):
            column = at // 2
            out_ref[level, :, 0, column : column + UNIT] = source[:, at : at + UNIT]
            out_ref[level, :, 1, column : column + UNIT] = source[:, at + UNIT : at + GROUP]


def small(kernel, shapes, place, *arrays):
    whole = pl.BlockSpec(memory_space=pltpu.VMEM)
    scalars = [] if place is None else [pl.BlockSpec(memory_space=pltpu.SMEM)]
    operands = arrays if place is None else (place, *arrays)
    return pl.pallas_call(
        kernel,
        out_shape=[jax.ShapeDtypeStruct(shape, jnp.float32) for shape in shapes],
        in_specs=scalars + [whole] * len(arrays),
        out_specs=[whole] * len(shapes),
        compiler_params=pltpu.CompilerParams(vmem_limit_bytes=16 * 2**20),
    )(*operands)


def on_device(
    loads, pivot_root, pivot_mid, pivot_low, upper_mid, upper_low, lower_mid, lower_low, index_maps
):
    levels, rows, _, columns = loads.shape
    leaf, core, row = lax.axis_index("leaf"), lax.axis_index("col"), lax.axis_index("row")
    cell = lax.axis_index(("row", "col"))
    far = leaf >> 3
    odd, high = far & 1 == 1, far & 2 == 2
    place = jnp.stack([leaf & NEAR - 1, far, row, core, leaf, cell]).astype(jnp.int32)
    barrier = lax.optimization_barrier

    def local(matrix):
        return matrix.reshape(2, -1, matrix.shape[-1])

    shapes = [(rows, 2 * columns), (2 * rows, columns), (2 * rows + 8, columns)]
    load_low, kept, gone = small(first_kernel, shapes, place, loads, index_maps)
    load_low, odd, high = barrier((load_low, odd, high))
    got = far_swapped(gone, 1)
    half = columns // 2
    shapes = [(2 * rows, columns), (2 * rows, 2 * rows), (2 * rows, half), (2 * rows + 8, half)]
    load_mid, low_mask, kept, gone = small(second_kernel, shapes, place, index_maps, kept, got)

    own_pivot, own_upper, own_lower = local(pivot_mid), local(upper_mid), local(lower_mid)
    root = local(pivot_root)
    got, own_pivot, root = barrier((got, own_pivot, root))
    far_pivot = far_swapped(own_pivot, 1)
    three_real, one_real = far_swapped(root[:1], 3), far_swapped(root[:1], 1)
    three_imag = far_swapped(root[1:], 3)

    inner_low = front_apply([[local(pivot_low)]], load_low, place, 1)
    ready = (inner_low, load_mid, far_pivot, three_real)
    inner_low, load_mid, far_pivot, three_real = barrier(ready)
    update_low = front_apply([[local(upper_low)]], inner_low, place, 1)
    update_low, one_real, three_imag = barrier((update_low, one_real, three_imag))
    stays, goes = lane_halves(update_low, odd)
    update = jnp.concatenate([stays, far_swapped(goes, 1)])
    right_mid = load_mid - routed(low_mask, update, 1)
    right_mid, late_root, one_real = barrier((right_mid, root[1:], one_real))
    one_imag, two_real = far_swapped(late_root, 1), far_swapped(one_real, 3)
    one_imag, own_upper = barrier((one_imag, own_upper))
    far_upper, two_imag = far_swapped(own_upper, 1), far_swapped(one_imag, 3)
    inner_mid = front_apply([[own_pivot], [far_pivot]], right_mid, place, 2)
    inner_mid, one_imag, two_real = barrier((inner_mid, one_imag, two_real))
    update_mid = front_apply([[own_upper], [far_upper]], inner_mid, place, 2)
    update_mid, two_imag = barrier((update_mid, two_imag))
    stays, goes = lane_halves(update_mid, high)
    got_root = far_swapped(jnp.concatenate([goes, gone]), 2)
    shapes = [(4 * rows, half), (4 * rows, 4 * rows)]
    load_root, root_mask = small(third_kernel, shapes, place, index_maps, kept, got, got_root)
    update = jnp.concatenate([stays, got_root[: 2 * rows]])
    right_root = load_root - routed(root_mask, update, 1)
    right_root, own_lower = barrier((right_root, own_lower))
    far_lower = far_swapped(own_lower, 1)
    inner_root = front_apply(
        [[root], [one_real, one_imag], [two_real, two_imag], [three_real, three_imag]], right_root, place, 4
    )
    inner_root, far_lower = barrier((inner_root, far_lower))

    z_root = routed(root_mask, inner_root, 0)
    own = jnp.concatenate([z_root[: 2 * rows], inner_root[: 2 * rows]])
    other = jnp.concatenate([z_root[2 * rows :], inner_root[2 * rows :]])
    halves = beside(own, far_swapped(other, 2), high)
    z_mid, root_half = halves[: 2 * rows], halves[2 * rows :]
    final_mid = inner_mid - front_apply([[own_lower], [far_lower]], z_mid, place, 2)

    z_half = routed(low_mask, final_mid, 0)
    own = jnp.concatenate([z_half[:rows], final_mid[:rows], root_half[:rows]])
    other = jnp.concatenate([z_half[rows:], final_mid[rows:], root_half[rows:]])
    wholes = beside(own, far_swapped(other, 1), odd)
    final_low = inner_low - front_apply([[local(lower_low)]], wholes[:rows], place, 1)
    finals = (wholes[2 * rows :], wholes[rows : 2 * rows], final_low)
    return small(last_kernel, [loads.shape], None, *finals)[0]


def solution(mesh):
    matrix = P(None, None, "row", "col", None, "leaf")
    vectors = P(None, ("leaf", "row", "col"), None, None)
    in_specs = (vectors,) + (matrix,) * 7 + (P(None, ("leaf", "row", "col")),)
    return jax.shard_map(
        on_device, mesh=mesh, in_specs=in_specs, out_specs=vectors, check_vma=False
    )
```

```python
import functools

import jax
import jax.numpy as jnp
from jax import lax
from jax.experimental import pallas as pl
from jax.experimental.pallas import tpu as pltpu
from jax.sharding import PartitionSpec as P

NEAR = 8
UNIT = 64
GROUP = 2 * UNIT


def core_swapped(shard):
    return lax.ppermute(shard, "col", [(0, 1), (1, 0)])


def far_swapped(shard, flip):
    return lax.ppermute(shard, "leaf", [(i, i ^ flip * NEAR) for i in range(lax.axis_size("leaf"))])


def near_block(block, step):
    count = lax.axis_size("leaf")
    pairs = [(i // NEAR * NEAR + (i + step) % NEAR, i) for i in range(count)]
    return lax.ppermute(block, "leaf", pairs)


def beside(own, other, upper):
    return jnp.where(
        upper,
        jnp.concatenate([other, own], axis=-1),
        jnp.concatenate([own, other], axis=-1),
    )


def lane_halves(block, upper):
    half = block.shape[-1] // 2
    lower, higher = block[..., :half], block[..., half:]
    return jnp.where(upper, higher, lower), jnp.where(upper, lower, higher)


def split(value):
    high = value.astype(jnp.bfloat16)
    return high, (value - high.astype(jnp.float32)).astype(jnp.bfloat16)


def dot(left, right):
    return lax.dot_general(
        left, right, (((0,), (0,)), ((), ())), preferred_element_type=jnp.float32
    )


def turned(value):
    parts = []
    for at in range(0, value.shape[1], GROUP):
        parts += [value[:, at + UNIT : at + GROUP], -value[:, at : at + UNIT]]
    return jnp.concatenate(parts, axis=1)


def apply_kernel(counts, place_ref, *refs):
    wide, pieces = len(counts), refs[:6]
    mine_ref, theirs_ref, vector, result = refs[-4:]
    starts = [6 + sum(counts[:flip]) for flip in range(wide)]
    near, far, row, core = (place_ref[i] for i in range(4))
    rows = vector.shape[0] // (wide * NEAR)
    steps = [(0, 0, 0), (1, 1, 0), (1, 3, 1), (2, 2, 0), (3, 4, 0), (4, 7, 0), (4, 5, 1), (5, 6, 0)]
    for piece, step, part in steps:
        block = (near + step) % NEAR
        for flip in range(wide):
            at = ((far ^ flip) % wide * NEAR + block) * rows
            base = (part * wide + flip) * rows
            vector[pl.ds(pl.multiple_of(at, rows), rows), :] = pieces[piece][base : base + rows, :]
    sums = [None] * wide
    straight = vector[...]
    for part, value in ((0, straight), (1, turned(straight))):
        high, low = split(value)
        for flip in range(wide):
            at = starts[flip]
            factor = refs[at][part] if counts[flip] == 1 else refs[at + part][0]
            top, rest = split(factor)
            lanes = high.shape[1]
            both = dot(top, jnp.concatenate([high, low], axis=1))
            term = both[:, :lanes] + both[:, lanes:] + dot(rest, high)
            sums[flip] = term if sums[flip] is None else sums[flip] + term
    for flip in range(wide):
        for at in range(8):
            result[at // 2, at % 2, flip * rows : (flip + 1) * rows, :] = sums[flip][
                at * rows : (at + 1) * rows
            ]
    for step in range(4):
        mine_ref[step] = result[(row + step) % 4, core]
        theirs_ref[step] = result[(row + step) % 4, 1 - core]


def local_apply(factors, pieces, place, wide):
    rows, lanes = pieces[0].shape
    whole = pl.BlockSpec(memory_space=pltpu.VMEM)
    counts = [len(factor) for factor in factors]
    arrays = [array for factor in factors for array in factor]
    return pl.pallas_call(
        functools.partial(apply_kernel, counts),
        out_shape=[jax.ShapeDtypeStruct((4, rows, lanes), jnp.float32)] * 2,
        in_specs=[pl.BlockSpec(memory_space=pltpu.SMEM)] + [whole] * (6 + len(arrays)),
        out_specs=[whole] * 2,
        scratch_shapes=[
            pltpu.VMEM((arrays[0].shape[1], lanes), jnp.float32),
            pltpu.VMEM((4, 2, rows, lanes), jnp.float32),
        ],
        compiler_params=pltpu.CompilerParams(vmem_limit_bytes=32 * 2**20),
    )(place, *pieces, *arrays)


def front_apply(factors, block, place, wide):
    above, below = near_block(block, 2), near_block(block, -2)
    up = near_block(jnp.concatenate([block, above]), 1)
    down = near_block(jnp.concatenate([block, below]), -1)
    across = near_block(above, 2)
    mine, theirs = local_apply(factors, [block, up, above, across, down, below], place, wide)
    summed = mine + core_swapped(theirs)
    rows = lax.axis_size("row")
    total = summed[0]
    for step in (1, 3, 2):
        total = total + lax.ppermute(
            summed[step], "row", [(i, (i + step) % rows) for i in range(rows)]
        )
    return total


def routed(mask, value, axis):
    return lax.dot_general(
        mask,
        value,
        (((axis,), (0,)), ((), ())),
        precision=lax.Precision.HIGH,
        preferred_element_type=jnp.float32,
    )


def chosen(upper, first, second):
    return jnp.where(jnp.full(first.shape, upper, jnp.int32) == 1, first, second)


def mask_into(mask_ref, entries, place_ref, group, flip):
    leaf, cell = place_ref[4], place_ref[5]
    size, rows = mask_ref.shape[0], entries[0].shape[1]
    every = lax.broadcasted_iota(jnp.int32, (size, rows), 0)
    for side, entry in enumerate(entries):
        own_block = lax.rem(leaf ^ side * NEAR, 2 * group) * 8 + cell
        target, slot = lax.div(entry, rows), lax.rem(entry, rows)
        at = jnp.where(target == own_block, side * rows, (side ^ flip) * rows) + slot
        hit = jnp.broadcast_to(at, (size, rows)) == every
        mask_ref[:, side * rows : (side + 1) * rows] = jnp.where(hit, 1.0, 0.0).astype(jnp.float32)


def first_kernel(place_ref, loads_ref, maps_ref, low_ref, kept_ref, gone_ref):
    rows, columns = loads_ref.shape[1], loads_ref.shape[3]
    odd = place_ref[1] & 1
    for level in range(3):
        real, imag = loads_ref[level, :, 0, :], loads_ref[level, :, 1, :]
        parts = []
        for at in range(0, columns, UNIT):
            parts += [real[:, at : at + UNIT], imag[:, at : at + UNIT]]
        whole = jnp.concatenate(parts, axis=1)
        if level == 2:
            low_ref[...] = whole
        else:
            lower, upper = whole[:, :columns], whole[:, columns:]
            kept_ref[level * rows : (level + 1) * rows, :] = chosen(odd, upper, lower)
            gone_ref[level * rows : (level + 1) * rows, :] = chosen(odd, lower, upper)
    gone_ref[2 * rows :, :] = jnp.zeros((8, columns), jnp.float32)
    gone_ref[2 * rows : 2 * rows + 2, :rows] = maps_ref[...].astype(jnp.float32)


def second_kernel(place_ref, maps_ref, kept_ref, got_ref, mid_ref, mask_ref, kept2_ref, gone_ref):
    rows, lanes = maps_ref.shape[1], kept_ref.shape[1] // 2
    high = place_ref[1] >> 1
    mid_ref[:rows, :] = kept_ref[rows:, :]
    mid_ref[rows:, :] = got_ref[rows : 2 * rows, :]
    other = got_ref[2 * rows : 2 * rows + 2, :rows].astype(jnp.int32)
    mask_into(mask_ref, [maps_ref[1:2, :], other[1:2]], place_ref, NEAR, 1)
    for half, source in enumerate((kept_ref, got_ref)):
        lower, upper = source[:rows, :lanes], source[:rows, lanes:]
        kept2_ref[half * rows : (half + 1) * rows, :] = chosen(high, upper, lower)
        gone_ref[half * rows : (half + 1) * rows, :] = chosen(high, lower, upper)
    gone_ref[2 * rows :, :] = jnp.zeros((8, lanes), jnp.float32)
    gone_ref[2 * rows : 2 * rows + 1, :rows] = maps_ref[0:1, :].astype(jnp.float32)
    gone_ref[2 * rows + 1 : 2 * rows + 2, :rows] = other[0:1].astype(jnp.float32)


def third_kernel(place_ref, maps_ref, kept_ref, got1_ref, got2_ref, root_ref, mask_ref):
    rows = maps_ref.shape[1]
    root_ref[: 2 * rows, :] = kept_ref[...]
    root_ref[2 * rows :, :] = got2_ref[2 * rows : 4 * rows, :]
    one = got1_ref[2 * rows : 2 * rows + 1, :rows].astype(jnp.int32)
    rest = got2_ref[4 * rows : 4 * rows + 2, :rows].astype(jnp.int32)
    entries = [maps_ref[0:1, :], one, rest[0:1], rest[1:2]]
    mask_into(mask_ref, entries, place_ref, 2 * NEAR, 2)


def last_kernel(root_ref, mid_ref, low_ref, out_ref):
    for level, source in enumerate((root_ref, mid_ref, low_ref)):
        for at in range(0, source.shape[1], GROUP):
            column = at // 2
            out_ref[level, :, 0, column : column + UNIT] = source[:, at : at + UNIT]
            out_ref[level, :, 1, column : column + UNIT] = source[:, at + UNIT : at + GROUP]


def small(kernel, shapes, place, *arrays):
    whole = pl.BlockSpec(memory_space=pltpu.VMEM)
    scalars = [] if place is None else [pl.BlockSpec(memory_space=pltpu.SMEM)]
    operands = arrays if place is None else (place, *arrays)
    return pl.pallas_call(
        kernel,
        out_shape=[jax.ShapeDtypeStruct(shape, jnp.float32) for shape in shapes],
        in_specs=scalars + [whole] * len(arrays),
        out_specs=[whole] * len(shapes),
        compiler_params=pltpu.CompilerParams(vmem_limit_bytes=16 * 2**20),
    )(*operands)


def on_device(
    loads, pivot_root, pivot_mid, pivot_low, upper_mid, upper_low, lower_mid, lower_low, index_maps
):
    levels, rows, _, columns = loads.shape
    leaf, core, row = lax.axis_index("leaf"), lax.axis_index("col"), lax.axis_index("row")
    cell = lax.axis_index(("row", "col"))
    far = leaf >> 3
    odd, high = far & 1 == 1, far & 2 == 2
    place = jnp.stack([leaf & NEAR - 1, far, row, core, leaf, cell]).astype(jnp.int32)
    barrier = lax.optimization_barrier

    def local(matrix):
        return matrix.reshape(2, -1, matrix.shape[-1])

    shapes = [(rows, 2 * columns), (2 * rows, columns), (2 * rows + 8, columns)]
    load_low, kept, gone = small(first_kernel, shapes, place, loads, index_maps)
    load_low, odd, high = barrier((load_low, odd, high))
    got = far_swapped(gone, 1)
    half = columns // 2
    shapes = [(2 * rows, columns), (2 * rows, 2 * rows), (2 * rows, half), (2 * rows + 8, half)]
    load_mid, low_mask, kept, gone = small(second_kernel, shapes, place, index_maps, kept, got)

    own_pivot, own_upper, own_lower = local(pivot_mid), local(upper_mid), local(lower_mid)
    root = local(pivot_root)
    got, own_pivot, root = barrier((got, own_pivot, root))
    far_pivot = far_swapped(own_pivot, 1)
    three_real, one_real = far_swapped(root[:1], 3), far_swapped(root[:1], 1)
    three_imag = far_swapped(root[1:], 3)

    inner_low = front_apply([[local(pivot_low)]], load_low, place, 1)
    ready = (inner_low, load_mid, far_pivot, three_real)
    inner_low, load_mid, far_pivot, three_real = barrier(ready)
    update_low = front_apply([[local(upper_low)]], inner_low, place, 1)
    update_low, one_real, three_imag = barrier((update_low, one_real, three_imag))
    stays, goes = lane_halves(update_low, odd)
    update = jnp.concatenate([stays, far_swapped(goes, 1)])
    right_mid = load_mid - routed(low_mask, update, 1)
    right_mid, late_root, one_real = barrier((right_mid, root[1:], one_real))
    one_imag, two_real = far_swapped(late_root, 1), far_swapped(one_real, 3)
    one_imag, own_upper = barrier((one_imag, own_upper))
    far_upper, two_imag = far_swapped(own_upper, 1), far_swapped(one_imag, 3)
    inner_mid = front_apply([[own_pivot], [far_pivot]], right_mid, place, 2)
    inner_mid, one_imag, two_real = barrier((inner_mid, one_imag, two_real))
    update_mid = front_apply([[own_upper], [far_upper]], inner_mid, place, 2)
    update_mid, two_imag = barrier((update_mid, two_imag))
    stays, goes = lane_halves(update_mid, high)
    got_root = far_swapped(jnp.concatenate([goes, gone]), 2)
    shapes = [(4 * rows, half), (4 * rows, 4 * rows)]
    load_root, root_mask = small(third_kernel, shapes, place, index_maps, kept, got, got_root)
    update = jnp.concatenate([stays, got_root[: 2 * rows]])
    right_root = load_root - routed(root_mask, update, 1)
    right_root, own_lower = barrier((right_root, own_lower))
    far_lower = far_swapped(own_lower, 1)
    inner_root = front_apply(
        [[root], [one_real, one_imag], [two_real, two_imag], [three_real, three_imag]], right_root, place, 4
    )
    inner_root, far_lower = barrier((inner_root, far_lower))

    z_root = routed(root_mask, inner_root, 0)
    own = jnp.concatenate([z_root[: 2 * rows], inner_root[: 2 * rows]])
    other = jnp.concatenate([z_root[2 * rows :], inner_root[2 * rows :]])
    halves = beside(own, far_swapped(other, 2), high)
    z_mid, root_half = halves[: 2 * rows], halves[2 * rows :]
    final_mid = inner_mid - front_apply([[own_lower], [far_lower]], z_mid, place, 2)

    z_half = routed(low_mask, final_mid, 0)
    own = jnp.concatenate([z_half[:rows], final_mid[:rows], root_half[:rows]])
    other = jnp.concatenate([z_half[rows:], final_mid[rows:], root_half[rows:]])
    wholes = beside(own, far_swapped(other, 1), odd)
    final_low = inner_low - front_apply([[local(lower_low)]], wholes[:rows], place, 1)
    finals = (wholes[2 * rows :], wholes[rows : 2 * rows], final_low)
    return small(last_kernel, [loads.shape], None, *finals)[0]


def solution(mesh):
    matrix = P(None, None, "row", "col", None, "leaf")
    vectors = P(None, ("leaf", "row", "col"), None, None)
    in_specs = (vectors,) + (matrix,) * 7 + (P(None, ("leaf", "row", "col")),)
    return jax.shard_map(
        on_device, mesh=mesh, in_specs=in_specs, out_specs=vectors, check_vma=False
    )
```
